512 devices in a mesh: row: 16 (over x, y_lo, core), col: 32 (over z, y_hi).
Axes of the slice: x: 4, y: 8 (y_hi: 4, y_lo: 2; y = y_hi * 2 + y_lo), z: 8, core: 2. Of those that a mesh axis runs over, the one named last changes fastest.
Arguments:
- iterate: bfloat16 [8192, 4096], P('row', 'col'), may hold values from -0.125 to 0.125
Outputs:
- update: bfloat16 [8192, 4096], P('row', 'col')
The draws below stay inside these ranges and needn't reach their ends.
All inputs are finite; a program needn't handle non-finite values.
Results may differ from the reference program's by a relative error of at most 0.0068.
Values may be sent and summed in bfloat16 or wider, within the bound.
A program may use at most 64 MiB of HBM per device.

```python
import math
import jax
import jax.numpy as jnp

N = 4096
ROWS = 8192


def raised(array, stream_key, source, target, shards_of, factor):
    owner, partner = [(jnp.arange(array.shape[dim]) // (array.shape[dim] // shards_of)).reshape([-1 if axis == dim else 1 for axis in range(array.ndim)]) for dim in (source, target)]
    chosen = jax.random.permutation(stream_key, shards_of)[partner]
    strong = (owner == chosen) | (owner == (partner + shards_of // 2) % shards_of)
    return jnp.where(strong, factor * array, array)


def block_scale(rng, extent, shards, least, top_value):
    gain, own = 1.0, jax.random.fold_in(rng, 6)
    for axis_at, blocks in shards:
        draws = jnp.exp(jax.random.uniform(jax.random.fold_in(own, axis_at), (blocks,), jnp.float32, least / len(shards), top_value / len(shards)))
        gain = gain * jnp.repeat(draws, extent[axis_at] // blocks).reshape([-1 if axis == axis_at else 1 for axis in range(len(extent))])
    return gain


def heavy_noise(own_key, dims, scale, bound, pieces, heavy, held_as=jnp.bfloat16):
    result = scale * jax.random.normal(own_key, dims, jnp.float32)
    if pieces:
        result = result * block_scale(own_key, dims, pieces, -0.22, 0.18)
    return jnp.clip(raised(result, jax.random.fold_in(own_key, 3), *heavy), -bound, bound).astype(held_as)


def setup_inputs(seed: int = 0) -> dict:
    seeds = jax.random.split(jax.random.key(seed), 2)
    return {
        "iterate": heavy_noise(seeds[0], (ROWS, N), ROWS ** -0.5, 0.125, ((0, 16), (1, 32)), (0, 1, 32, 2.75)),
    }


def reference(iterate):
    gram_block = jnp.dot(iterate.T, iterate, preferred_element_type=jnp.float32)
    gram_half = gram_block.astype(jnp.bfloat16)
    first_term = jnp.dot(iterate, gram_half, preferred_element_type=jnp.float32)
    first_half = first_term.astype(jnp.bfloat16)
    second_term = jnp.dot(first_half, gram_half, preferred_element_type=jnp.float32)
    update_scale = 0.2 * math.sqrt(max(ROWS, N))
    mixed = 3.4445 * iterate.astype(jnp.float32) - 4.775 * first_term + 2.0315 * second_term
    return (update_scale * mixed).astype(jnp.bfloat16)
```

```python
import math

import jax
import jax.numpy as jnp
from jax import lax
from jax.experimental import pallas as pl
from jax.experimental.pallas import tpu as pltpu
from jax.sharding import PartitionSpec as P

MESH = pl.DeviceIdType.MESH
BF16 = jnp.bfloat16
F32 = jnp.float32

R, W = 512, 128
NZ, NY = 8, 4
GATHER_CHUNKS = 2
ROW_CHUNKS = 4
SLABS = [(dx, dy) for dx in range(4) for dy in range(2) if (dx, dy) != (0, 0)]
SCALE = 0.2 * math.sqrt(8192)


class Copies:
    def __init__(self, send_sems, recv_sems):
        self.send_sems, self.recv_sems, self.used, self.started = send_sems, recv_sems, 0, []

    def make(self, src, dst, device):
        at = self.used
        self.used += 1
        return pltpu.make_async_remote_copy(
            src_ref=src,
            dst_ref=dst,
            send_sem=self.send_sems.at[at],
            recv_sem=self.recv_sems.at[at],
            device_id=device,
            device_id_type=MESH,
        )

    def start(self, src, dst, device):
        copy = self.make(src, dst, device)
        copy.start()
        self.started.append(copy)
        return copy


def tdot(left, right):
    return lax.dot_general(left, right, (((0,), (0,)), ((), ())), preferred_element_type=F32)


def ring_plan(chunks):
    order = []
    for t in range(1, 5 + chunks):
        for c in range(chunks):
            k = t - c
            if 1 <= k <= 3:
                order += [(k, c), (NZ - k, c)]
            elif k == 4:
                order.append((4, c))
    return order


def kernel(x_ref, o_ref, xa, xb, xao, xbo, gp, rb, g, sa, ra, sb, rbb, ah, acc, send_sems, recv_sems):
    r, c_ = lax.axis_index("row"), lax.axis_index("col")
    x, yl, q = r // 4, (r // 2) % 2, r % 2
    z, yh = c_ // 4, c_ % 4
    slab = x * 2 + yl
    sibling = (x * 4 + yl * 2 + (1 - q), c_)
    z_up = (r, ((z + 1) % NZ) * 4 + yh)
    z_down = (r, ((z + NZ - 1) % NZ) * 4 + yh)
    y_dev = {e: (r, z * 4 + (yh + e) % NY) for e in range(1, NY)}
    slab_of = {}
    slab_dev = {}
    slab_from = {}
    for dx, dy in SLABS:
        tx, ty = (x + dx) % 4, (yl + dy) % 2
        slab_of[dx, dy] = tx * 2 + ty
        slab_dev[dx, dy] = (tx * 4 + ty * 2 + q, c_)
        slab_from[dx, dy] = ((x + 4 - dx) % 4) * 2 + (yl + dy) % 2

    barrier = pltpu.get_barrier_semaphore()
    partners = [sibling, z_up, z_down] + list(y_dev.values()) + list(slab_dev.values())
    for device in partners:
        pl.semaphore_signal(barrier, inc=1, device_id=device, device_id_type=MESH)
    pl.semaphore_wait(barrier, len(partners))

    cps = Copies(send_sems, recv_sems)

    def cols(ref, at, rows=None):
        return ref.at[:, pl.ds(at * W, W)] if rows is None else ref.at[rows, pl.ds(at * W, W)]

    def chunk_rows(c, chunks):
        return pl.ds(c * (R // chunks), R // chunks)

    def forward(buf, k, c, chunks, first=None):
        rows = chunk_rows(c, chunks)
        src = cols(buf, k, rows) if first is None else first.at[rows, :]
        got = []
        if k <= 3 and (k < 3 or c % 2 == 0):
            got.append((k + 1, c, cps.start(src, cols(buf, k + 1, rows), z_down)))
        if (k == 0 or k >= 5) and (k != 5 or c % 2 == 1):
            m = (k + NZ - 1) % NZ
            got.append((m, c, cps.start(src, cols(buf, m, rows), z_up)))
        return got

    arrive = {}
    for c in range(GATHER_CHUNKS):
        for k, cc, copy in forward(xa, 0, c, GATHER_CHUNKS, x_ref):
            arrive[k, cc] = copy
    y_in = {}
    for e in (1, 3, 2):
        y_in[NY - e] = cps.start(x_ref, cols(xb, NY - e), y_dev[e])
    sib_in = [cps.start(x_ref, cols(xbo, 0), sibling)]
    xa[:, 0:W] = x_ref[...]
    xb[:, 0:W] = x_ref[...]

    half_in = []

    def to_sibling(k, c):
        rows = chunk_rows(c, GATHER_CHUNKS)
        copy = cps.make(cols(xa, k, rows), cols(xao, k % 4, rows), sibling)
        half_in.append((k // 4, copy))

        @pl.when(q != k // 4)
        def _():
            copy.start()

    for c in range(GATHER_CHUNKS):
        to_sibling(0, c)
    order = ring_plan(GATHER_CHUNKS)
    for n, (k, c) in enumerate(order):
        arrive[k, c].wait_recv()
        for kk, cc, copy in forward(xa, k, c, GATHER_CHUNKS) if k != 4 else []:
            arrive[kk, cc] = copy
        to_sibling(k, c)
    for e in (1, 3, 2):
        y_in[e].wait_recv()
        sib_in.append(cps.start(cols(xb, e), cols(xbo, e), sibling))
    for copy in sib_in:
        copy.wait_recv()
    for owner, copy in half_in:

        @pl.when(q == owner)
        def _(copy=copy):
            copy.wait_recv()

    for i in range(4):
        at = pl.multiple_of(q * (4 * W) + i * W, W)
        part = tdot(xa[:, pl.ds(at, W)], xb[...])
        part += tdot(xao[:, i * W : (i + 1) * W], xbo[...])
        half = part.astype(BF16)
        gp[2 * i] = half[:64]
        gp[2 * i + 1] = half[64:]

    rs_in = []
    for j, d in enumerate(SLABS):
        rs_in.append(cps.start(gp.at[slab_of[d]], rb.at[j], slab_dev[d]))
    total = gp[slab].astype(F32)
    for j, copy in enumerate(rs_in):
        copy.wait_recv()
        total += rb[j].astype(F32)
    half_rows = q * (4 * W)

    def piece(w):
        return g.at[pl.ds(pl.multiple_of(half_rows + w * 64, 64), 64), :]

    piece(slab)[...] = total.astype(BF16)
    ag_in = []
    for d in SLABS:
        ag_in.append((d, cps.start(piece(slab), piece(slab), slab_dev[d])))
    g_in = [cps.start(piece(slab), piece(slab), sibling)]
    for d, copy in ag_in:
        copy.wait_recv()
        g_in.append(cps.start(piece(slab_from[d]), piece(slab_from[d]), sibling))
    for copy in g_in:
        copy.wait_recv()

    RC = R // ROW_CHUNKS
    a_in = {}
    for c in range(ROW_CHUNKS):
        rows = pl.ds(c * RC, RC)
        part = jnp.dot(xa[rows, :], g[...], preferred_element_type=F32)
        acc[rows, :] = part[:, :W]
        for e in (1, 3, 2):
            sa[rows, e * W : (e + 1) * W] = part[:, e * W : (e + 1) * W].astype(BF16)
            a_in[NY - e, c] = cps.start(cols(sa, e, rows), cols(ra, NY - e, rows), y_dev[e])

    a_arrive, b_in = {}, {}

    def finish_first(c):
        rows = pl.ds(c * RC, RC)
        first = acc[rows, :]
        for e in (1, 3, 2):
            a_in[e, c].wait_recv()
            first += ra[rows, e * W : (e + 1) * W].astype(F32)
        acc[rows, :] = first
        ah[rows, 0:W] = first.astype(BF16)
        for k, cc, copy in forward(ah, 0, c, ROW_CHUNKS):
            a_arrive[k, cc] = copy

    def second_product(c):
        rows = pl.ds(c * RC, RC)
        part = jnp.dot(ah[rows, :], g[...], preferred_element_type=F32)
        for e in (1, 3, 2):
            sb[rows, e * W : (e + 1) * W] = part[:, e * W : (e + 1) * W].astype(BF16)
            b_in[NY - e, c] = cps.start(
                cols(sb, e, rows), cols(rbb, NY - e, rows), y_dev[e]
            )
        mixed = 3.4445 * x_ref[rows, :].astype(F32) - 4.775 * acc[rows, :]
        acc[rows, :] = mixed + 2.0315 * part[:, :W]

    for t in range(ROW_CHUNKS + 5):
        for c in range(ROW_CHUNKS):
            k = t - c
            if k == 0:
                finish_first(c)
            for kk in {1: (1, 7), 2: (2, 6), 3: (3, 5), 4: (4,)}.get(k, ()):
                a_arrive[kk, c].wait_recv()
                for k2, c2, copy in forward(ah, kk, c, ROW_CHUNKS) if kk != 4 else []:
                    a_arrive[k2, c2] = copy
            if k == 4:
                second_product(c)

    for c in range(ROW_CHUNKS):
        rows = pl.ds(c * RC, RC)
        second = jnp.zeros((RC, W), F32)
        for e in (1, 3, 2):
            b_in[e, c].wait_recv()
            second += rbb[rows, e * W : (e + 1) * W].astype(F32)
        o_ref[rows, :] = (SCALE * (acc[rows, :] + 2.0315 * second)).astype(BF16)

    for copy in cps.started:
        copy.wait_send()
    for owner, copy in half_in:

        @pl.when(q != owner)
        def _(copy=copy):
            copy.wait_send()


COPIES = 160


def body(iterate):
    vmem = pl.BlockSpec(memory_space=pltpu.VMEM)
    return pl.pallas_call(
        kernel,
        out_shape=jax.ShapeDtypeStruct((R, W), BF16),
        in_specs=[vmem],
        out_specs=vmem,
        scratch_shapes=[
            pltpu.VMEM((R, NZ * W), BF16),
            pltpu.VMEM((R, NY * W), BF16),
            pltpu.VMEM((R, 4 * W), BF16),
            pltpu.VMEM((R, NY * W), BF16),
            pltpu.VMEM((8, 64, NY * W), BF16),
            pltpu.VMEM((7, 64, NY * W), BF16),
            pltpu.VMEM((NZ * W, NY * W), BF16),
            pltpu.VMEM((R, NY * W), BF16),
            pltpu.VMEM((R, NY * W), BF16),
            pltpu.VMEM((R, NY * W), BF16),
            pltpu.VMEM((R, NY * W), BF16),
            pltpu.VMEM((R, NZ * W), BF16),
            pltpu.VMEM((R, W), F32),
            pltpu.SemaphoreType.DMA((COPIES,)),
            pltpu.SemaphoreType.DMA((COPIES,)),
        ],
        compiler_params=pltpu.CompilerParams(
            collective_id=0, has_side_effects=True, vmem_limit_bytes=32 << 20
        ),
        name="newton_schulz",
    )(iterate)


def solution(mesh):
    placed = (P("row", "col"),)
    return jax.shard_map(
        body, mesh=mesh, in_specs=placed, out_specs=P("row", "col"), check_vma=False
    )
```

```python
import math

import jax
import jax.numpy as jnp
from jax import lax
from jax.experimental import pallas as pl
from jax.experimental.pallas import tpu as pltpu
from jax.sharding import PartitionSpec as P

MESH = pl.DeviceIdType.MESH
BF16 = jnp.bfloat16
F32 = jnp.float32

R, W = 512, 128
NZ, NY = 8, 4
U = 256
V = R - U
PARTS = 2
SLABS = [(dx, dy) for dx in (2, 1, 3, 0) for dy in (1, 0) if (dx, dy) != (0, 0)]
SCALE = 0.2 * math.sqrt(8192)
PLACE = {d: i for i, d in enumerate((0, 1, 7, 2, 6, 3, 5, 4))}
GRAM_CHUNKS = ((0, 5), (5, 8))


def tdot(left, right):
    return lax.dot_general(left, right, (((0,), (0,)), ((), ())), preferred_element_type=F32)


def kernel(
    x_hbm, o_ref, x_ref, xa, xb, xao, xbo, gp, rb, g, su1, ru1, su2, ru2, ov1, rv1, fv1, ov2, rv2, fv2, ah, av, kept, through, acc,
    load_sem, send_sems, recv_sems,
):
    r, c_ = lax.axis_index("row"), lax.axis_index("col")
    x, yl, q = r // 4, (r // 2) % 2, r % 2
    z, yh = c_ // 4, c_ % 4
    slab = x * 2 + yl
    sibling = (x * 4 + yl * 2 + (1 - q), c_)
    z_dev = {d: (r, ((z + d) % NZ) * 4 + yh) for d in (1, 2, 6, 7)}
    y_dev = {e: (r, z * 4 + (yh + e) % NY) for e in range(1, NY)}
    slab_of, slab_dev, slab_from = {}, {}, {}
    for dx, dy in SLABS:
        tx, ty = (x + dx) % 4, (yl + dy) % 2
        slab_of[dx, dy] = tx * 2 + ty
        slab_dev[dx, dy] = (tx * 4 + ty * 2 + q, c_)
        slab_from[dx, dy] = ((x + 4 - dx) % 4) * 2 + ty

    load = pltpu.make_async_copy(x_hbm, x_ref, load_sem)
    load.start()
    barrier = pltpu.get_barrier_semaphore()
    partners = [sibling] + list(z_dev.values()) + list(y_dev.values()) + list(slab_dev.values())
    for device in partners:
        pl.semaphore_signal(barrier, inc=1, device_id=device, device_id_type=MESH)
    load.wait()
    xa[:, 0:W] = x_ref[...]
    xb[:, 0:W] = x_ref[...]
    pl.semaphore_wait(barrier, len(partners))

    started = []

    def send(src, dst, device):
        at = len(started)
        copy = pltpu.make_async_remote_copy(
            src_ref=src,
            dst_ref=dst,
            send_sem=send_sems.at[at],
            recv_sem=recv_sems.at[at],
            device_id=device,
            device_id_type=MESH,
        )
        copy.start()
        started.append(copy)
        return copy

    def slot(ref, at, first=0, count=R):
        return ref.at[pl.ds(first, count), pl.ds(at * W, W)]

    def z_near(src, buf, first, count):
        got = {}
        for d in (2, 6, 1, 7):
            got[(NZ - d) % NZ] = send(src, slot(buf, PLACE[(NZ - d) % NZ], first, count), z_dev[d])
        return got

    def z_far(buf, d, first, count, got):
        step = 7 if d == 2 else 1
        twice = 6 if d == 2 else 2
        far = 3 if d == 2 else 5
        here = slot(buf, PLACE[d], first, count)
        got[far] = send(here, slot(buf, PLACE[far], first, count), z_dev[step])
        half = first if d == 2 else first + count // 2
        got[4, d] = send(
            slot(buf, PLACE[d], half, count // 2), slot(buf, PLACE[4], half, count // 2), z_dev[twice]
        )

    z_in = {}
    PART = R // PARTS
    for near in ((2, 6), (1, 7)):
        for p in range(PARTS):
            for d in near:
                src = x_ref.at[pl.ds(p * PART, PART), :]
                z_in[NZ - d, p] = send(src, slot(xa, PLACE[NZ - d], p * PART, PART), z_dev[d])
    y_in = {NY - e: send(x_ref, slot(xb, NY - e), y_dev[e]) for e in (2, 1, 3)}
    xa_in = {0: send(x_ref, slot(xao, 0), sibling)}
    xb_in = {0: send(x_ref, slot(xbo, 0), sibling)}

    def pass_xa(d):
        xa_in[d] = send(slot(xa, PLACE[d]), slot(xao, PLACE[d]), sibling)

    far_in = [{} for _ in range(PARTS)]
    for p in range(PARTS):
        for d in (2, 6):
            z_in[d, p].wait_recv()
            z_far(xa, d, p * PART, PART, far_in[p])
    pass_xa(2)
    pass_xa(6)
    for d in (1, 7):
        for p in range(PARTS):
            z_in[d, p].wait_recv()
        pass_xa(d)
    for e in (1, 3, 2):
        y_in[e].wait_recv()
        xb_in[e] = send(slot(xb, e), slot(xbo, e), sibling)
    for e in (0, 1, 3, 2):
        xb_in[e].wait_recv()

    own = pl.ds(pl.multiple_of(q * (2 * W), 2 * W), 2 * W)

    def gram_rows(chunk):
        first, last = GRAM_CHUNKS[chunk]
        for at in range(first, last):
            part = tdot(xa[:, at * W : (at + 1) * W], xb[:, own])
            part += tdot(xao[:, at * W : (at + 1) * W], xbo[:, own])
            gp[at * W : (at + 1) * W, :] = part.astype(BF16)

    def piece(chunk, w):
        first, last = GRAM_CHUNKS[chunk]
        rows = (last - first) * (W // 8)
        return pl.ds(pl.multiple_of(first * W + w * rows, 16), rows)

    def reduce_start(chunk):
        first, last = GRAM_CHUNKS[chunk]
        rows = (last - first) * (W // 8)
        got = []
        for j, d in enumerate(SLABS):
            dst = rb.at[j, pl.ds(first * (W // 8), rows), :]
            got.append((j, send(gp.at[piece(chunk, slab_of[d]), :], dst, slab_dev[d])))
        return got

    def reduce_finish(chunk, got):
        first, last = GRAM_CHUNKS[chunk]
        mine = piece(chunk, slab)
        total = gp[mine, :].astype(F32)
        for j, copy in got:
            copy.wait_recv()
            total += rb[j, first * (W // 8) : last * (W // 8), :].astype(F32)
        g[mine, own] = total.astype(BF16)
        here = g.at[mine, own]
        gather = [(piece(chunk, slab_from[d]), send(here, here, slab_dev[d])) for d in SLABS]
        return gather, [send(here, here, sibling)]

    def gather_finish(gather, both):
        for rows, copy in gather:
            copy.wait_recv()
            here = g.at[rows, own]
            both.append(send(here, here, sibling))

    for d in (0, 2, 6, 1, 7):
        xa_in[d].wait_recv()
    gram_rows(0)
    reduce_0 = reduce_start(0)
    for d in (3, 5):
        for p in range(PARTS):
            far_in[p][d].wait_recv()
        pass_xa(d)
    for p in range(PARTS):
        for d in (2, 6):
            far_in[p][4, d].wait_recv()
    pass_xa(4)
    for d in (3, 5, 4):
        xa_in[d].wait_recv()
    gram_rows(1)
    reduce_1 = reduce_start(1)
    gather_0, both_0 = reduce_finish(0, reduce_0)
    gather_1, both_1 = reduce_finish(1, reduce_1)
    gather_finish(gather_0, both_0)
    gather_finish(gather_1, both_1)
    for copy in both_0 + both_1:
        copy.wait_recv()

    def u_product(rows_of, out, into):
        got = {}
        high = jnp.dot(rows_of[:U, :], g[:, 2 * W :], preferred_element_type=F32).astype(BF16)
        for e in (2, 3):
            out[:, e * W : (e + 1) * W] = high[:, (e - 2) * W : (e - 1) * W]
            got[NY - e] = send(slot(out, e, 0, U), slot(into, NY - e, 0, U), y_dev[e])
        low = jnp.dot(rows_of[:U, :], g[:, : 2 * W], preferred_element_type=F32)
        out[:, W : 2 * W] = low[:, W:].astype(BF16)
        got[3] = send(slot(out, 1, 0, U), slot(into, 3, 0, U), y_dev[1])
        return low[:, :W], got

    def u_sum(total, into, got):
        for e in (1, 3, 2):
            got[e].wait_recv()
            total += into[:, e * W : (e + 1) * W].astype(F32)
        return total

    def v_product(left, out, relay, into):
        part = lax.dot_general(
            left, g[...], (((1,), (1,)), ((), ())), preferred_element_type=F32
        )
        out[...] = part.astype(BF16)
        got = {}
        half = V // 2
        for n, d, first in ((2, 2, 0), (3, 6, half)):
            got[n] = send(slot(out, PLACE[4], first, half), relay.at[n, pl.ds(0, half), :], z_dev[d])
        for n, d, far in ((0, 1, 3), (1, 7, 5)):
            got[n] = send(slot(out, PLACE[far], 0, V), relay.at[n], z_dev[d])
        near = [send(slot(out, PLACE[d], 0, V), into.at[n], z_dev[d]) for n, d in ((0, 1), (1, 7))]
        for n, d in ((0, 2), (1, 6)):
            kept[n] = part[:, PLACE[d] * W : (PLACE[d] + 1) * W]
        return part[:, :W], got, near

    def v_relay(stage, relay, into, got, near):
        half = V // 2
        for n, d in ((0, 2), (1, 6)):
            got[n].wait_recv()
            total = kept[n] + relay[n].astype(F32)
            got[n + 2].wait_recv()
            more = relay[n + 2, :half, :].astype(F32)
            through[stage, n, :half] = (total[:half] + more if n == 0 else total[:half]).astype(BF16)
            through[stage, n, half:] = (total[half:] + more if n == 1 else total[half:]).astype(BF16)
            near.append(send(through.at[stage, n], into.at[n + 2], z_dev[d]))

    def v_sum(total, into, near):
        for n, copy in enumerate(near):
            copy.wait_recv()
            total += into[n].astype(F32)
        return total

    def mix(rows, first):
        return 3.4445 * x_ref[rows, :].astype(F32) - 4.775 * first

    urows, vrows = slice(0, U), slice(U, R)
    v_own, v_far, v_near = v_product(xb[vrows, :], ov1, rv1, fv1)
    acc[vrows, :] = v_own
    u_own, u_in = u_product(xa, su1, ru1)
    acc[urows, :] = u_own

    v_relay(0, rv1, fv1, v_far, v_near)
    first = u_sum(acc[urows, :], ru1, u_in)
    ah[:, 0:W] = first.astype(BF16)
    ah_in = z_near(slot(ah, 0, 0, U), ah, 0, U)
    acc[urows, :] = mix(urows, first)
    first = v_sum(acc[vrows, :], fv1, v_near)
    av[:, 0:W] = first.astype(BF16)
    av_in = [send(slot(av, 0, 0, V), slot(av, NY - e, 0, V), y_dev[e]) for e in (2, 1, 3)]
    acc[vrows, :] = mix(vrows, first)
    for d in (2, 6):
        ah_in[d].wait_recv()
        z_far(ah, d, 0, U, ah_in)
    for copy in av_in:
        copy.wait_recv()
    v_own, v_far, v_near = v_product(av[...], ov2, rv2, fv2)
    acc[vrows, :] += 2.0315 * v_own
    for d in (1, 7, 3, 5, (4, 2), (4, 6)):
        ah_in[d].wait_recv()
    u_own, u_in = u_product(ah, su2, ru2)
    acc[urows, :] += 2.0315 * u_own
    v_relay(1, rv2, fv2, v_far, v_near)
    second = u_sum(jnp.zeros((U, W), F32), ru2, u_in)
    o_ref[urows, :] = (SCALE * (acc[urows, :] + 2.0315 * second)).astype(BF16)
    second = v_sum(jnp.zeros((V, W), F32), fv2, v_near)
    o_ref[vrows, :] = (SCALE * (acc[vrows, :] + 2.0315 * second)).astype(BF16)

    for copy in started:
        copy.wait_send()


COPIES = 128


def body(iterate):
    return pl.pallas_call(
        kernel,
        out_shape=jax.ShapeDtypeStruct((R, W), BF16),
        in_specs=[pl.BlockSpec(memory_space=pl.ANY)],
        out_specs=pl.BlockSpec(memory_space=pltpu.VMEM),
        scratch_shapes=[
            pltpu.VMEM((R, W), BF16),
            pltpu.VMEM((R, NZ * W), BF16),
            pltpu.VMEM((R, NY * W), BF16),
            pltpu.VMEM((R, NZ * W), BF16),
            pltpu.VMEM((R, NY * W), BF16),
            pltpu.VMEM((NZ * W, 2 * W), BF16),
            pltpu.VMEM((7, NZ * W // 8, 2 * W), BF16),
            pltpu.VMEM((NZ * W, NY * W), BF16),
            pltpu.VMEM((U, NY * W), BF16),
            pltpu.VMEM((U, NY * W), BF16),
            pltpu.VMEM((U, NY * W), BF16),
            pltpu.VMEM((U, NY * W), BF16),
            pltpu.VMEM((V, NZ * W), BF16),
            pltpu.VMEM((4, V, W), BF16),
            pltpu.VMEM((4, V, W), BF16),
            pltpu.VMEM((V, NZ * W), BF16),
            pltpu.VMEM((4, V, W), BF16),
            pltpu.VMEM((4, V, W), BF16),
            pltpu.VMEM((U, NZ * W), BF16),
            pltpu.VMEM((V, NY * W), BF16),
            pltpu.VMEM((2, V, W), F32),
            pltpu.VMEM((2, 2, V, W), BF16),
            pltpu.VMEM((R, W), F32),
            pltpu.SemaphoreType.DMA,
            pltpu.SemaphoreType.DMA((COPIES,)),
            pltpu.SemaphoreType.DMA((COPIES,)),
        ],
        compiler_params=pltpu.CompilerParams(
            collective_id=0, has_side_effects=True, vmem_limit_bytes=32 << 20
        ),
        name="newton_schulz",
    )(iterate)


def solution(mesh):
    placed = (P("row", "col"),)
    return jax.shard_map(
        body, mesh=mesh, in_specs=placed, out_specs=P("row", "col"), check_vma=False
    )
```

```python
import math

import jax
import jax.numpy as jnp
from jax import lax
from jax.experimental import pallas as pl
from jax.experimental.pallas import tpu as pltpu
from jax.sharding import PartitionSpec as P

MESH = pl.DeviceIdType.MESH
BF16 = jnp.bfloat16
F32 = jnp.float32

R, W = 512, 128
NZ, NY = 8, 4
PARTS = 4
LAG = 1
U_CHUNKS = 4
V_CHUNKS = 4
Z_PLAN = ((0, 2), (0, 1), (2, 3), (2, 4))
SLABS = [(dx, dy) for dx in (2, 1, 3, 0) for dy in (1, 0) if (dx, dy) != (0, 0)]
SCALE = 0.2 * math.sqrt(8192)
ORDER = (0, 1, 7, 2, 6, 3, 5, 4)
PLACE = {d: i for i, d in enumerate(ORDER)}
GRAM_CHUNKS = ((0, 3), (3, 8))


def tdot(left, right):
    return lax.dot_general(left, right, (((0,), (0,)), ((), ())), preferred_element_type=F32)


def kernel(
    x_hbm, o_ref, x_ref, xa, xb, xao, xbo, gp, rb, g, su1, ru1, su2, ru2, ov1, rv1, fv1, ov2, rv2, fv2, ah, av, kept, through, acc,
    load_sem, send_sems, recv_sems,
):
    r, c_ = lax.axis_index("row"), lax.axis_index("col")
    x, yl, q = r // 4, (r // 2) % 2, r % 2
    z, yh = c_ // 4, c_ % 4
    slab = x * 2 + yl
    sibling = (x * 4 + yl * 2 + (1 - q), c_)
    z_dev = {d: (r, ((z + d) % NZ) * 4 + yh) for d in (1, 2, 6, 7)}
    y_dev = {e: (r, z * 4 + (yh + e) % NY) for e in range(1, NY)}
    slab_of, slab_dev, slab_from = {}, {}, {}
    for dx, dy in SLABS:
        tx, ty = (x + dx) % 4, (yl + dy) % 2
        slab_of[dx, dy] = tx * 2 + ty
        slab_dev[dx, dy] = (tx * 4 + ty * 2 + q, c_)
        slab_from[dx, dy] = ((x + 4 - dx) % 4) * 2 + ty

    load = pltpu.make_async_copy(x_hbm, x_ref, load_sem)
    load.start()
    barrier = pltpu.get_barrier_semaphore()
    partners = [sibling] + list(z_dev.values()) + list(y_dev.values()) + list(slab_dev.values())
    for device in partners:
        pl.semaphore_signal(barrier, inc=1, device_id=device, device_id_type=MESH)
    load.wait()
    xa[:, 0:W] = x_ref[...]
    xb[:, 0:W] = x_ref[...]
    pl.semaphore_wait(barrier, len(partners))

    started = []

    def send(src, dst, device):
        at = len(started)
        copy = pltpu.make_async_remote_copy(
            src_ref=src,
            dst_ref=dst,
            send_sem=send_sems.at[at],
            recv_sem=recv_sems.at[at],
            device_id=device,
            device_id_type=MESH,
        )
        copy.start()
        started.append(copy)
        return copy

    settled, mark = [0], [0]

    def settle():
        for copy in started[settled[0] : mark[0]]:
            copy.wait_send()
        settled[0], mark[0] = mark[0], len(started)

    def slot(ref, at, first=0, count=R):
        return ref.at[pl.ds(first, count), pl.ds(at * W, W)]

    def z_near(src, buf, first, count):
        got = {}
        for d in (2, 6, 1, 7):
            got[(NZ - d) % NZ] = send(src, slot(buf, PLACE[(NZ - d) % NZ], first, count), z_dev[d])
        return got

    def z_far(buf, d, first, count, got):
        step = 7 if d == 2 else 1
        twice = 6 if d == 2 else 2
        far = 3 if d == 2 else 5
        here = slot(buf, PLACE[d], first, count)
        got[far] = send(here, slot(buf, PLACE[far], first, count), z_dev[step])
        half = first if d == 2 else first + count // 2
        got[4, d] = send(
            slot(buf, PLACE[d], half, count // 2), slot(buf, PLACE[4], half, count // 2), z_dev[twice]
        )

    z_in, z_seen = {}, set()

    def z_wait(d):
        for key, copy in z_in.items():
            if key[0] == d and key not in z_seen:
                z_seen.add(key)
                copy.wait_recv()

    PART = R // PARTS

    def z_hop(near, target):
        for p in range(PARTS):
            for side in (1, -1):
                key = (near * side % NZ, p)
                if near and key not in z_seen:
                    z_seen.add(key)
                    z_in[key].wait_recv()
                hop = z_dev[-side * (target - near) % NZ]
                rows, key = (p * PART, PART), (target * side % NZ, p)
                if target == 4:
                    rows = (p * PART + (0 if side == 1 else PART // 2), PART // 2)
                    key = (4, p, side)
                src = slot(xa, PLACE[near * side % NZ], *rows) if near else x_ref.at[pl.ds(*rows), :]
                z_in[key] = send(src, slot(xa, PLACE[target * side % NZ], *rows), hop)

    for near, target in Z_PLAN:
        if near == 0:
            z_hop(near, target)
    y_in = {NY - e: send(x_ref, slot(xb, NY - e), y_dev[e]) for e in (2, 1, 3)}
    xa_in = {0: send(x_ref, slot(xao, 0), sibling)}
    xb_in = {0: send(x_ref, slot(xbo, 0), sibling)}

    def pass_xa(d):
        xa_in[d] = send(slot(xa, PLACE[d]), slot(xao, PLACE[d]), sibling)

    for near, target in Z_PLAN:
        if near:
            z_hop(near, target)
    for d in (1, 7, 2, 6):
        z_wait(d)
        pass_xa(d)
    for e in (1, 3, 2):
        y_in[e].wait_recv()
        xb_in[e] = send(slot(xb, e), slot(xbo, e), sibling)
    for e in (0, 1, 3, 2):
        xb_in[e].wait_recv()

    own = pl.ds(pl.multiple_of(q * (2 * W), 2 * W), 2 * W)

    def gram_rows(chunk):
        first, last = GRAM_CHUNKS[chunk]
        for at in range(first, last):
            part = tdot(xa[:, at * W : (at + 1) * W], xb[:, own])
            part += tdot(xao[:, at * W : (at + 1) * W], xbo[:, own])
            gp[at * W : (at + 1) * W, :] = part.astype(BF16)

    def piece(chunk, w):
        first, last = GRAM_CHUNKS[chunk]
        rows = (last - first) * (W // 8)
        return pl.ds(pl.multiple_of(first * W + w * rows, 16), rows)

    def reduce_start(chunk):
        first, last = GRAM_CHUNKS[chunk]
        rows = (last - first) * (W // 8)
        got = []
        for j, d in enumerate(SLABS):
            dst = rb.at[j, pl.ds(first * (W // 8), rows), :]
            got.append((j, send(gp.at[piece(chunk, slab_of[d]), :], dst, slab_dev[d])))
        return got

    def reduce_finish(chunk, got):
        first, last = GRAM_CHUNKS[chunk]
        mine = piece(chunk, slab)
        total = gp[mine, :].astype(F32)
        for j, copy in got:
            copy.wait_recv()
            total += rb[j, first * (W // 8) : last * (W // 8), :].astype(F32)
        g[mine, own] = total.astype(BF16)
        here = g.at[mine, own]
        gather = [(piece(chunk, slab_from[d]), send(here, here, slab_dev[d])) for d in SLABS]
        return gather, [send(here, here, sibling)]

    def gather_finish(gather, both):
        for rows, copy in gather:
            copy.wait_recv()
            here = g.at[rows, own]
            both.append(send(here, here, sibling))

    reduces, gathers = [], []
    for chunk, (first, last) in enumerate(GRAM_CHUNKS):
        for d in ORDER[first:last]:
            if d in (3, 4, 5):
                z_wait(d)
                pass_xa(d)
        for d in ORDER[first:last]:
            xa_in[d].wait_recv()
        gram_rows(chunk)
        reduces.append(reduce_start(chunk))
        if chunk >= LAG:
            gathers.append(reduce_finish(chunk - LAG, reduces[chunk - LAG]))
    settle()
    for chunk in range(len(GRAM_CHUNKS) - LAG, len(GRAM_CHUNKS)):
        gathers.append(reduce_finish(chunk, reduces[chunk]))
    settle()
    for gather, both in gathers:
        gather_finish(gather, both)
    for gather, both in gathers:
        for copy in both:
            copy.wait_recv()

    def u_product(rows_of, rows, out, into):
        first, count = rows
        got = {}
        left = rows_of[first : first + count, :]
        high = jnp.dot(left, g[:, 2 * W :], preferred_element_type=F32).astype(BF16)
        for e in (2, 3):
            out[first : first + count, e * W : (e + 1) * W] = high[:, (e - 2) * W : (e - 1) * W]
            got[NY - e] = send(slot(out, e, *rows), slot(into, NY - e, *rows), y_dev[e])
        low = jnp.dot(left, g[:, : 2 * W], preferred_element_type=F32)
        out[first : first + count, W : 2 * W] = low[:, W:].astype(BF16)
        got[3] = send(slot(out, 1, *rows), slot(into, 3, *rows), y_dev[1])
        return low[:, :W], got

    def u_sum(total, rows, into, got):
        first, count = rows
        for e in (1, 3, 2):
            got[e].wait_recv()
            total += into[first : first + count, e * W : (e + 1) * W].astype(F32)
        return total

    def v_product(left, rows, out, relay, into):
        first, count = rows[0], rows[1]
        part = lax.dot_general(
            left, g[...], (((1,), (1,)), ((), ())), preferred_element_type=F32
        )
        out[first : first + count, :] = part.astype(BF16)
        got = {}
        half = count // 2
        for n, d, start in ((2, 2, first), (3, 6, first + half)):
            src = slot(out, PLACE[4], start, half)
            got[n] = send(src, relay.at[n, pl.ds(first, half), :], z_dev[d])
        for n, d, far in ((0, 1, 3), (1, 7, 5)):
            src = slot(out, PLACE[far], first, count)
            got[n] = send(src, relay.at[n, pl.ds(first, count), :], z_dev[d])
        near = []
        for n, d in ((0, 1), (1, 7)):
            src = slot(out, PLACE[d], first, count)
            near.append(send(src, into.at[n, pl.ds(first, count), :], z_dev[d]))
        for n, d in ((0, 2), (1, 6)):
            kept[n, first : first + count] = part[:, PLACE[d] * W : (PLACE[d] + 1) * W]
        return part[:, :W], got, near

    def v_relay(stage, rows, relay, into, got, near):
        first, count = rows[0], rows[1]
        half = count // 2
        top, low = slice(first, first + half), slice(first + half, first + count)
        for n, d in ((0, 2), (1, 6)):
            got[n].wait_recv()
            got[n + 2].wait_recv()
            more = relay[n + 2, top, :].astype(F32)
            for part in (top, low):
                total = kept[n, part] + relay[n, part, :].astype(F32)
                if (part is top) == (n == 0):
                    total += more
                through[stage, n, part] = total.astype(BF16)
            src = through.at[stage, n, pl.ds(first, count), :]
            near.append(send(src, into.at[n + 2, pl.ds(first, count), :], z_dev[d]))

    def v_sum(total, rows, into, near):
        first, count = rows[0], rows[1]
        for n, copy in enumerate(near):
            copy.wait_recv()
            total += into[n, first : first + count, :].astype(F32)
        return total

    def of(rows):
        return slice(rows[0], rows[0] + rows[1])

    def mix(rows, first):
        return 3.4445 * x_ref[of(rows), :].astype(F32) - 4.775 * first

    def chunks(start, count, number):
        return [(start + n * (count // number), count // number) for n in range(number)]

    state = settled[0], mark[0], list(started)

    @pl.when(q == 0)
    def _():
        us = chunks(0, R, U_CHUNKS)
        u_in, ah_in = {}, {}
        for rows in us:
            acc[of(rows), :], u_in[rows] = u_product(xa, rows, su1, ru1)
        settle()
        for rows in us:
            first = u_sum(acc[of(rows), :], rows, ru1, u_in[rows])
            ah[of(rows), 0:W] = first.astype(BF16)
            ah_in[rows] = z_near(slot(ah, 0, *rows), ah, *rows)
            acc[of(rows), :] = mix(rows, first)
        settle()
        for rows in us:
            for d in (2, 6):
                ah_in[rows][d].wait_recv()
                z_far(ah, d, *rows, ah_in[rows])
        for rows in us:
            for d in (1, 7, 3, 5, (4, 2), (4, 6)):
                ah_in[rows][d].wait_recv()
            own_term, u_in[rows] = u_product(ah, rows, su2, ru2)
            acc[of(rows), :] += 2.0315 * own_term
        settle()
        for rows in us:
            second = u_sum(jnp.zeros((rows[1], W), F32), rows, ru2, u_in[rows])
            o_ref[of(rows), :] = (SCALE * (acc[of(rows), :] + 2.0315 * second)).astype(BF16)
        settle()
        settle()

    settled[0], mark[0] = state[:2]
    started[:] = state[2]

    @pl.when(q == 1)
    def _():
        vs = chunks(0, R, V_CHUNKS)
        v_in, av_in = {}, {}
        for rows in vs:
            acc[of(rows), :], *v_in[rows] = v_product(xb[of(rows), :], rows, ov1, rv1, fv1)
        settle()
        for rows in vs:
            v_relay(0, rows, rv1, fv1, *v_in[rows])
        for rows in vs:
            first = v_sum(acc[of(rows), :], rows, fv1, v_in[rows][1])
            av[of(rows), 0:W] = first.astype(BF16)
            av_in[rows] = [
                send(slot(av, 0, *rows), slot(av, NY - e, *rows), y_dev[e]) for e in (2, 1, 3)
            ]
            acc[of(rows), :] = mix(rows, first)
        settle()
        for rows in vs:
            for copy in av_in[rows]:
                copy.wait_recv()
            own_term, *v_in[rows] = v_product(av[of(rows), :], rows, ov2, rv2, fv2)
            acc[of(rows), :] += 2.0315 * own_term
        settle()
        for rows in vs:
            v_relay(1, rows, rv2, fv2, *v_in[rows])
        for rows in vs:
            second = v_sum(jnp.zeros((rows[1], W), F32), rows, fv2, v_in[rows][1])
            o_ref[of(rows), :] = (SCALE * (acc[of(rows), :] + 2.0315 * second)).astype(BF16)
        settle()
        settle()


COPIES = 192


def body(iterate):
    return pl.pallas_call(
        kernel,
        out_shape=jax.ShapeDtypeStruct((R, W), BF16),
        in_specs=[pl.BlockSpec(memory_space=pl.ANY)],
        out_specs=pl.BlockSpec(memory_space=pltpu.VMEM),
        scratch_shapes=[
            pltpu.VMEM((R, W), BF16),
            pltpu.VMEM((R, NZ * W), BF16),
            pltpu.VMEM((R, NY * W), BF16),
            pltpu.VMEM((R, NZ * W), BF16),
            pltpu.VMEM((R, NY * W), BF16),
            pltpu.VMEM((NZ * W, 2 * W), BF16),
            pltpu.VMEM((7, NZ * W // 8, 2 * W), BF16),
            pltpu.VMEM((NZ * W, NY * W), BF16),
            pltpu.VMEM((R, NY * W), BF16),
            pltpu.VMEM((R, NY * W), BF16),
            pltpu.VMEM((R, NY * W), BF16),
            pltpu.VMEM((R, NY * W), BF16),
            pltpu.VMEM((R, NZ * W), BF16),
            pltpu.VMEM((4, R, W), BF16),
            pltpu.VMEM((4, R, W), BF16),
            pltpu.VMEM((R, NZ * W), BF16),
            pltpu.VMEM((4, R, W), BF16),
            pltpu.VMEM((4, R, W), BF16),
            pltpu.VMEM((R, NZ * W), BF16),
            pltpu.VMEM((R, NY * W), BF16),
            pltpu.VMEM((2, R, W), F32),
            pltpu.VMEM((2, 2, R, W), BF16),
            pltpu.VMEM((R, W), F32),
            pltpu.SemaphoreType.DMA,
            pltpu.SemaphoreType.DMA((COPIES,)),
            pltpu.SemaphoreType.DMA((COPIES,)),
        ],
        compiler_params=pltpu.CompilerParams(
            collective_id=0, has_side_effects=True, vmem_limit_bytes=32 << 20
        ),
        name="newton_schulz",
    )(iterate)


def solution(mesh):
    placed = (P("row", "col"),)
    return jax.shard_map(
        body, mesh=mesh, in_specs=placed, out_specs=P("row", "col"), check_vma=False
    )
```

```python
import math

import jax
import jax.numpy as jnp
from jax import lax
from jax.experimental import pallas as pl
from jax.experimental.pallas import tpu as pltpu
from jax.sharding import PartitionSpec as P

MESH = pl.DeviceIdType.MESH
BF16 = jnp.bfloat16
F32 = jnp.float32

R, W = 512, 128
NZ, NY = 8, 4
PARTS = 4
LAG = 1
U_CHUNKS = 4
V_CHUNKS = 4
Z_PLAN = ((0, 2), (0, 1), (2, 3), (2, 4))
SLABS = [(dx, dy) for dx in (2, 1, 3, 0) for dy in (1, 0) if (dx, dy) != (0, 0)]
SCALE = 0.2 * math.sqrt(8192)
ORDER = (0, 1, 7, 2, 6, 3, 5, 4)
PLACE = {d: i for i, d in enumerate(ORDER)}
GRAM_CHUNKS = ((0, 5), (5, 8))


def tdot(left, right):
    return lax.dot_general(left, right, (((0,), (0,)), ((), ())), preferred_element_type=F32)


def kernel(
    x_hbm, o_ref, x_ref, xa, xb, xao, xbo, gp, rb, g, su1, ru1, su2, ru2, ov1, rv1, fv1, ov2, rv2, fv2, ah, av, kept, through, acc,
    load_sem, send_sems, recv_sems,
):
    r, c_ = lax.axis_index("row"), lax.axis_index("col")
    x, yl, q = r // 4, (r // 2) % 2, r % 2
    z, yh = c_ // 4, c_ % 4
    slab = x * 2 + yl
    sibling = (x * 4 + yl * 2 + (1 - q), c_)
    z_dev = {d: (r, ((z + d) % NZ) * 4 + yh) for d in (1, 2, 6, 7)}
    y_dev = {e: (r, z * 4 + (yh + e) % NY) for e in range(1, NY)}
    slab_of, slab_dev, slab_from = {}, {}, {}
    for dx, dy in SLABS:
        tx, ty = (x + dx) % 4, (yl + dy) % 2
        slab_of[dx, dy] = tx * 2 + ty
        slab_dev[dx, dy] = (tx * 4 + ty * 2 + q, c_)
        slab_from[dx, dy] = ((x + 4 - dx) % 4) * 2 + ty

    load = pltpu.make_async_copy(x_hbm, x_ref, load_sem)
    load.start()
    barrier = pltpu.get_barrier_semaphore()
    partners = [sibling] + list(z_dev.values()) + list(y_dev.values()) + list(slab_dev.values())
    for device in partners:
        pl.semaphore_signal(barrier, inc=1, device_id=device, device_id_type=MESH)
    load.wait()
    xa[:, 0:W] = x_ref[...]
    xb[:, 0:W] = x_ref[...]
    pl.semaphore_wait(barrier, len(partners))

    started = []

    def send(src, dst, device):
        at = len(started)
        copy = pltpu.make_async_remote_copy(
            src_ref=src,
            dst_ref=dst,
            send_sem=send_sems.at[at],
            recv_sem=recv_sems.at[at],
            device_id=device,
            device_id_type=MESH,
        )
        copy.start()
        started.append(copy)
        return copy

    settled, mark = [0], [0]

    def settle():
        for copy in started[settled[0] : mark[0]]:
            copy.wait_send()
        settled[0], mark[0] = mark[0], len(started)

    def slot(ref, at, first=0, count=R):
        return ref.at[pl.ds(first, count), pl.ds(at * W, W)]

    def z_near(src, buf, first, count):
        got = {}
        for d in (2, 6, 1, 7):
            got[(NZ - d) % NZ] = send(src, slot(buf, PLACE[(NZ - d) % NZ], first, count), z_dev[d])
        return got

    def z_far(buf, d, first, count, got):
        step = 7 if d == 2 else 1
        twice = 6 if d == 2 else 2
        far = 3 if d == 2 else 5
        here = slot(buf, PLACE[d], first, count)
        got[far] = send(here, slot(buf, PLACE[far], first, count), z_dev[step])
        half = first if d == 2 else first + count // 2
        got[4, d] = send(
            slot(buf, PLACE[d], half, count // 2), slot(buf, PLACE[4], half, count // 2), z_dev[twice]
        )

    z_in, z_seen = {}, set()

    def z_wait(d):
        for key, copy in z_in.items():
            if key[0] == d and key not in z_seen:
                z_seen.add(key)
                copy.wait_recv()

    PART = R // PARTS

    def z_hop(near, target):
        for p in range(PARTS):
            for side in (1, -1):
                key = (near * side % NZ, p)
                if near and key not in z_seen:
                    z_seen.add(key)
                    z_in[key].wait_recv()
                hop = z_dev[-side * (target - near) % NZ]
                rows, key = (p * PART, PART), (target * side % NZ, p)
                if target == 4:
                    rows = (p * PART + (0 if side == 1 else PART // 2), PART // 2)
                    key = (4, p, side)
                src = slot(xa, PLACE[near * side % NZ], *rows) if near else x_ref.at[pl.ds(*rows), :]
                z_in[key] = send(src, slot(xa, PLACE[target * side % NZ], *rows), hop)

    for near, target in Z_PLAN:
        if near == 0:
            z_hop(near, target)
    y_in = {NY - e: send(x_ref, slot(xb, NY - e), y_dev[e]) for e in (2, 1, 3)}
    xa_in = {0: send(x_ref, slot(xao, 0), sibling)}
    xb_in = {0: send(x_ref, slot(xbo, 0), sibling)}

    def pass_xa(d):
        xa_in[d] = send(slot(xa, PLACE[d]), slot(xao, PLACE[d]), sibling)

    for near, target in Z_PLAN:
        if near:
            z_hop(near, target)
    for d in (1, 7, 2, 6):
        z_wait(d)
        pass_xa(d)
    for e in (1, 3, 2):
        y_in[e].wait_recv()
        xb_in[e] = send(slot(xb, e), slot(xbo, e), sibling)
    for e in (0, 1, 3, 2):
        xb_in[e].wait_recv()

    own = pl.ds(pl.multiple_of(q * (2 * W), 2 * W), 2 * W)

    def gram_rows(chunk):
        first, last = GRAM_CHUNKS[chunk]
        for at in range(first, last):
            part = tdot(xa[:, at * W : (at + 1) * W], xb[:, own])
            part += tdot(xao[:, at * W : (at + 1) * W], xbo[:, own])
            gp[at * W : (at + 1) * W, :] = part.astype(BF16)

    def piece(chunk, w):
        first, last = GRAM_CHUNKS[chunk]
        rows = (last - first) * (W // 8)
        return pl.ds(pl.multiple_of(first * W + w * rows, 16), rows)

    def reduce_start(chunk):
        first, last = GRAM_CHUNKS[chunk]
        rows = (last - first) * (W // 8)
        got = []
        for j, d in enumerate(SLABS):
            dst = rb.at[j, pl.ds(first * (W // 8), rows), :]
            got.append((j, send(gp.at[piece(chunk, slab_of[d]), :], dst, slab_dev[d])))
        return got

    def reduce_finish(chunk, got):
        first, last = GRAM_CHUNKS[chunk]
        mine = piece(chunk, slab)
        total = gp[mine, :].astype(F32)
        for j, copy in got:
            copy.wait_recv()
            total += rb[j, first * (W // 8) : last * (W // 8), :].astype(F32)
        g[mine, own] = total.astype(BF16)
        here = g.at[mine, own]
        gather = [(piece(chunk, slab_from[d]), send(here, here, slab_dev[d])) for d in SLABS]
        return gather, [send(here, here, sibling)]

    def gather_finish(gather, both):
        for rows, copy in gather:
            copy.wait_recv()
            here = g.at[rows, own]
            both.append(send(here, here, sibling))

    reduces, gathers = [], []
    for chunk, (first, last) in enumerate(GRAM_CHUNKS):
        for d in ORDER[first:last]:
            if d in (3, 4, 5):
                z_wait(d)
                pass_xa(d)
        for d in ORDER[first:last]:
            xa_in[d].wait_recv()
        gram_rows(chunk)
        reduces.append(reduce_start(chunk))
        if chunk >= LAG:
            gathers.append(reduce_finish(chunk - LAG, reduces[chunk - LAG]))
    settle()
    for chunk in range(len(GRAM_CHUNKS) - LAG, len(GRAM_CHUNKS)):
        gathers.append(reduce_finish(chunk, reduces[chunk]))
    settle()
    for gather, both in gathers:
        gather_finish(gather, both)
    for gather, both in gathers:
        for copy in both:
            copy.wait_recv()

    def u_product(rows_of, rows, out, into):
        first, count = rows
        got = {}
        left = rows_of[first : first + count, :]
        high = jnp.dot(left, g[:, 2 * W :], preferred_element_type=F32).astype(BF16)
        for e in (2, 3):
            out[first : first + count, e * W : (e + 1) * W] = high[:, (e - 2) * W : (e - 1) * W]
            got[NY - e] = send(slot(out, e, *rows), slot(into, NY - e, *rows), y_dev[e])
        low = jnp.dot(left, g[:, : 2 * W], preferred_element_type=F32)
        out[first : first + count, W : 2 * W] = low[:, W:].astype(BF16)
        got[3] = send(slot(out, 1, *rows), slot(into, 3, *rows), y_dev[1])
        return low[:, :W], got

    def u_sum(total, rows, into, got):
        first, count = rows
        for e in (1, 3, 2):
            got[e].wait_recv()
            total += into[first : first + count, e * W : (e + 1) * W].astype(F32)
        return total

    def v_product(left, rows, out, relay, into):
        first, count = rows[0], rows[1]
        part = lax.dot_general(
            left, g[...], (((1,), (1,)), ((), ())), preferred_element_type=F32
        )
        out[first : first + count, :] = part.astype(BF16)
        got = {}
        half = count // 2
        for n, d, start in ((2, 2, first), (3, 6, first + half)):
            src = slot(out, PLACE[4], start, half)
            got[n] = send(src, relay.at[n, pl.ds(first, half), :], z_dev[d])
        for n, d, far in ((0, 1, 3), (1, 7, 5)):
            src = slot(out, PLACE[far], first, count)
            got[n] = send(src, relay.at[n, pl.ds(first, count), :], z_dev[d])
        near = []
        for n, d in ((0, 1), (1, 7)):
            src = slot(out, PLACE[d], first, count)
            near.append(send(src, into.at[n, pl.ds(first, count), :], z_dev[d]))
        for n, d in ((0, 2), (1, 6)):
            kept[n, first : first + count] = part[:, PLACE[d] * W : (PLACE[d] + 1) * W]
        return part[:, :W], got, near

    def v_relay(stage, rows, relay, into, got, near):
        first, count = rows[0], rows[1]
        half = count // 2
        top, low = slice(first, first + half), slice(first + half, first + count)
        for n, d in ((0, 2), (1, 6)):
            got[n].wait_recv()
            got[n + 2].wait_recv()
            more = relay[n + 2, top, :].astype(F32)
            for part in (top, low):
                total = kept[n, part] + relay[n, part, :].astype(F32)
                if (part is top) == (n == 0):
                    total += more
                through[stage, n, part] = total.astype(BF16)
            src = through.at[stage, n, pl.ds(first, count), :]
            near.append(send(src, into.at[n + 2, pl.ds(first, count), :], z_dev[d]))

    def v_sum(total, rows, into, near):
        first, count = rows[0], rows[1]
        for n, copy in enumerate(near):
            copy.wait_recv()
            total += into[n, first : first + count, :].astype(F32)
        return total

    def of(rows):
        return slice(rows[0], rows[0] + rows[1])

    def mix(rows, first):
        return 3.4445 * x_ref[of(rows), :].astype(F32) - 4.775 * first

    def chunks(start, count, number):
        return [(start + n * (count // number), count // number) for n in range(number)]

    state = settled[0], mark[0], list(started)

    @pl.when(q == 0)
    def _():
        us = chunks(0, R, U_CHUNKS)
        u_in, ah_in = {}, {}
        for rows in us:
            acc[of(rows), :], u_in[rows] = u_product(xa, rows, su1, ru1)
        settle()
        for rows in us:
            first = u_sum(acc[of(rows), :], rows, ru1, u_in[rows])
            ah[of(rows), 0:W] = first.astype(BF16)
            ah_in[rows] = z_near(slot(ah, 0, *rows), ah, *rows)
            acc[of(rows), :] = mix(rows, first)
        settle()
        for rows in us:
            for d in (2, 6):
                ah_in[rows][d].wait_recv()
                z_far(ah, d, *rows, ah_in[rows])
        for rows in us:
            for d in (1, 7, 3, 5, (4, 2), (4, 6)):
                ah_in[rows][d].wait_recv()
            own_term, u_in[rows] = u_product(ah, rows, su2, ru2)
            acc[of(rows), :] += 2.0315 * own_term
        settle()
        for rows in us:
            second = u_sum(jnp.zeros((rows[1], W), F32), rows, ru2, u_in[rows])
            o_ref[of(rows), :] = (SCALE * (acc[of(rows), :] + 2.0315 * second)).astype(BF16)
        settle()
        settle()

    settled[0], mark[0] = state[:2]
    started[:] = state[2]

    @pl.when(q == 1)
    def _():
        vs = chunks(0, R, V_CHUNKS)
        v_in, av_in = {}, {}
        for rows in vs:
            acc[of(rows), :], *v_in[rows] = v_product(xb[of(rows), :], rows, ov1, rv1, fv1)
        settle()
        for rows in vs:
            v_relay(0, rows, rv1, fv1, *v_in[rows])
        for rows in vs:
            first = v_sum(acc[of(rows), :], rows, fv1, v_in[rows][1])
            av[of(rows), 0:W] = first.astype(BF16)
            av_in[rows] = [
                send(slot(av, 0, *rows), slot(av, NY - e, *rows), y_dev[e]) for e in (2, 1, 3)
            ]
            acc[of(rows), :] = mix(rows, first)
        settle()
        for rows in vs:
            for copy in av_in[rows]:
                copy.wait_recv()
            own_term, *v_in[rows] = v_product(av[of(rows), :], rows, ov2, rv2, fv2)
            acc[of(rows), :] += 2.0315 * own_term
        settle()
        for rows in vs:
            v_relay(1, rows, rv2, fv2, *v_in[rows])
        for rows in vs:
            second = v_sum(jnp.zeros((rows[1], W), F32), rows, fv2, v_in[rows][1])
            o_ref[of(rows), :] = (SCALE * (acc[of(rows), :] + 2.0315 * second)).astype(BF16)
        settle()
        settle()


COPIES = 192


def body(iterate):
    return pl.pallas_call(
        kernel,
        out_shape=jax.ShapeDtypeStruct((R, W), BF16),
        in_specs=[pl.BlockSpec(memory_space=pl.ANY)],
        out_specs=pl.BlockSpec(memory_space=pltpu.VMEM),
        scratch_shapes=[
            pltpu.VMEM((R, W), BF16),
            pltpu.VMEM((R, NZ * W), BF16),
            pltpu.VMEM((R, NY * W), BF16),
            pltpu.VMEM((R, NZ * W), BF16),
            pltpu.VMEM((R, NY * W), BF16),
            pltpu.VMEM((NZ * W, 2 * W), BF16),
            pltpu.VMEM((7, NZ * W // 8, 2 * W), BF16),
            pltpu.VMEM((NZ * W, NY * W), BF16),
            pltpu.VMEM((R, NY * W), BF16),
            pltpu.VMEM((R, NY * W), BF16),
            pltpu.VMEM((R, NY * W), BF16),
            pltpu.VMEM((R, NY * W), BF16),
            pltpu.VMEM((R, NZ * W), BF16),
            pltpu.VMEM((4, R, W), BF16),
            pltpu.VMEM((4, R, W), BF16),
            pltpu.VMEM((R, NZ * W), BF16),
            pltpu.VMEM((4, R, W), BF16),
            pltpu.VMEM((4, R, W), BF16),
            pltpu.VMEM((R, NZ * W), BF16),
            pltpu.VMEM((R, NY * W), BF16),
            pltpu.VMEM((2, R, W), F32),
            pltpu.VMEM((2, 2, R, W), BF16),
            pltpu.VMEM((R, W), F32),
            pltpu.SemaphoreType.DMA,
            pltpu.SemaphoreType.DMA((COPIES,)),
            pltpu.SemaphoreType.DMA((COPIES,)),
        ],
        compiler_params=pltpu.CompilerParams(
            collective_id=0, has_side_effects=True, vmem_limit_bytes=32 << 20
        ),
        name="newton_schulz",
    )(iterate)


def solution(mesh):
    placed = (P("row", "col"),)
    return jax.shard_map(
        body, mesh=mesh, in_specs=placed, out_specs=P("row", "col"), check_vma=False
    )
```

```python
import math

import jax
import jax.numpy as jnp
from jax import lax
from jax.experimental import pallas as pl
from jax.experimental.pallas import tpu as pltpu
from jax.sharding import PartitionSpec as P

MESH = pl.DeviceIdType.MESH
BF16 = jnp.bfloat16
F32 = jnp.float32

R, W = 512, 128
NZ, NY = 8, 4
PARTS = 4
LAG = 1
U_CHUNKS = 4
V_CHUNKS = 4
Z_PLAN = ((0, 2), (0, 1), (2, 3), (2, 4))
SLABS = [(dx, dy) for dx in (2, 1, 3, 0) for dy in (1, 0) if (dx, dy) != (0, 0)]
SCALE = 0.2 * math.sqrt(8192)
ORDER = (0, 1, 7, 2, 6, 3, 5, 4)
PLACE = {d: i for i, d in enumerate(ORDER)}
GRAM_CHUNKS = ((0, 5), (5, 8))


def tdot(left, right):
    return lax.dot_general(left, right, (((0,), (0,)), ((), ())), preferred_element_type=F32)


def kernel(
    x_hbm, o_ref, x_ref, xa, xb, xao, xbo, gp, rb, g, su1, ru1, su2, ru2, ov1, rv1, fv1, ov2, rv2, fv2, ah, av, kept, through, acc,
    load_sem, send_sems, recv_sems,
):
    r, c_ = lax.axis_index("row"), lax.axis_index("col")
    x, yl, q = r // 4, (r // 2) % 2, r % 2
    z, yh = c_ // 4, c_ % 4
    slab = x * 2 + yl
    sibling = (x * 4 + yl * 2 + (1 - q), c_)
    z_dev = {d: (r, ((z + d) % NZ) * 4 + yh) for d in (1, 2, 6, 7)}
    y_dev = {e: (r, z * 4 + (yh + e) % NY) for e in range(1, NY)}
    slab_of, slab_dev, slab_from = {}, {}, {}
    for dx, dy in SLABS:
        tx, ty = (x + dx) % 4, (yl + dy) % 2
        slab_of[dx, dy] = tx * 2 + ty
        slab_dev[dx, dy] = (tx * 4 + ty * 2 + q, c_)
        slab_from[dx, dy] = ((x + 4 - dx) % 4) * 2 + ty

    load = pltpu.make_async_copy(x_hbm, x_ref, load_sem)
    load.start()
    barrier = pltpu.get_barrier_semaphore()
    partners = [sibling] + list(z_dev.values()) + list(y_dev.values()) + list(slab_dev.values())
    for device in partners:
        pl.semaphore_signal(barrier, inc=1, device_id=device, device_id_type=MESH)
    load.wait()
    xa[:, 0:W] = x_ref[...]
    xb[:, 0:W] = x_ref[...]
    pl.semaphore_wait(barrier, len(partners))

    started = []

    def send(src, dst, device):
        at = len(started)
        copy = pltpu.make_async_remote_copy(
            src_ref=src,
            dst_ref=dst,
            send_sem=send_sems.at[at],
            recv_sem=recv_sems.at[at],
            device_id=device,
            device_id_type=MESH,
        )
        copy.start()
        started.append(copy)
        return copy

    settled, mark = [0], [0]

    def settle():
        for copy in started[settled[0] : mark[0]]:
            copy.wait_send()
        settled[0], mark[0] = mark[0], len(started)

    def slot(ref, at, first=0, count=R):
        return ref.at[pl.ds(first, count), pl.ds(at * W, W)]

    def z_near(src, buf, first, count):
        got = {}
        for d in (2, 6, 1, 7):
            got[(NZ - d) % NZ] = send(src, slot(buf, PLACE[(NZ - d) % NZ], first, count), z_dev[d])
        return got

    def z_far(buf, d, first, count, got):
        step = 7 if d == 2 else 1
        twice = 6 if d == 2 else 2
        far = 3 if d == 2 else 5
        here = slot(buf, PLACE[d], first, count)
        got[far] = send(here, slot(buf, PLACE[far], first, count), z_dev[step])
        half = first if d == 2 else first + count // 2
        got[4, d] = send(
            slot(buf, PLACE[d], half, count // 2), slot(buf, PLACE[4], half, count // 2), z_dev[twice]
        )

    z_in, z_seen = {}, set()

    def z_wait(d):
        for key, copy in z_in.items():
            if key[0] == d and key not in z_seen:
                z_seen.add(key)
                copy.wait_recv()

    PART = R // PARTS

    def z_hop(near, target):
        for p in range(PARTS):
            for side in (1, -1):
                key = (near * side % NZ, p)
                if near and key not in z_seen:
                    z_seen.add(key)
                    z_in[key].wait_recv()
                hop = z_dev[-side * (target - near) % NZ]
                rows, key = (p * PART, PART), (target * side % NZ, p)
                if target == 4:
                    rows = (p * PART + (0 if side == 1 else PART // 2), PART // 2)
                    key = (4, p, side)
                src = slot(xa, PLACE[near * side % NZ], *rows) if near else x_ref.at[pl.ds(*rows), :]
                z_in[key] = send(src, slot(xa, PLACE[target * side % NZ], *rows), hop)

    for near, target in Z_PLAN:
        if near == 0:
            z_hop(near, target)
    y_in = {NY - e: send(x_ref, slot(xb, NY - e), y_dev[e]) for e in (2, 1, 3)}
    xa_in = {0: send(x_ref, slot(xao, 0), sibling)}
    xb_in = {0: send(x_ref, slot(xbo, 0), sibling)}

    def pass_xa(d):
        xa_in[d] = send(slot(xa, PLACE[d]), slot(xao, PLACE[d]), sibling)

    for near, target in Z_PLAN:
        if near:
            z_hop(near, target)
    for d in (1, 7, 2, 6):
        z_wait(d)
        pass_xa(d)
    for e in (1, 3, 2):
        y_in[e].wait_recv()
        xb_in[e] = send(slot(xb, e), slot(xbo, e), sibling)
    for e in (0, 1, 3, 2):
        xb_in[e].wait_recv()

    own = pl.ds(pl.multiple_of(q * (2 * W), 2 * W), 2 * W)

    def gram_rows(chunk):
        first, last = GRAM_CHUNKS[chunk]
        for at in range(first, last):
            part = tdot(xa[:, at * W : (at + 1) * W], xb[:, own])
            part += tdot(xao[:, at * W : (at + 1) * W], xbo[:, own])
            gp[at * W : (at + 1) * W, :] = part.astype(BF16)

    def piece(chunk, w):
        first, last = GRAM_CHUNKS[chunk]
        rows = (last - first) * (W // 8)
        return pl.ds(pl.multiple_of(first * W + w * rows, 16), rows)

    def reduce_start(chunk):
        first, last = GRAM_CHUNKS[chunk]
        rows = (last - first) * (W // 8)
        got = []
        for j, d in enumerate(SLABS):
            dst = rb.at[j, pl.ds(first * (W // 8), rows), :]
            got.append((j, send(gp.at[piece(chunk, slab_of[d]), :], dst, slab_dev[d])))
        return got

    def reduce_finish(chunk, got):
        first, last = GRAM_CHUNKS[chunk]
        mine = piece(chunk, slab)
        total = gp[mine, :].astype(F32)
        for j, copy in got:
            copy.wait_recv()
            total += rb[j, first * (W // 8) : last * (W // 8), :].astype(F32)
        g[mine, own] = total.astype(BF16)
        here = g.at[mine, own]
        gather = [(piece(chunk, slab_from[d]), send(here, here, slab_dev[d])) for d in SLABS]
        return gather, [send(here, here, sibling)]

    def gather_finish(gather, both):
        for rows, copy in gather:
            copy.wait_recv()
            here = g.at[rows, own]
            both.append(send(here, here, sibling))

    reduces, gathers = [], []
    for chunk, (first, last) in enumerate(GRAM_CHUNKS):
        for d in ORDER[first:last]:
            if d in (3, 4, 5):
                z_wait(d)
                pass_xa(d)
        for d in ORDER[first:last]:
            xa_in[d].wait_recv()
        gram_rows(chunk)
        reduces.append(reduce_start(chunk))
        if chunk >= LAG:
            gathers.append(reduce_finish(chunk - LAG, reduces[chunk - LAG]))
    settle()
    for chunk in range(len(GRAM_CHUNKS) - LAG, len(GRAM_CHUNKS)):
        gathers.append(reduce_finish(chunk, reduces[chunk]))
    settle()
    for gather, both in gathers:
        gather_finish(gather, both)
    for gather, both in gathers:
        for copy in both:
            copy.wait_recv()

    def u_product(rows_of, rows, out, into):
        first, count = rows
        got = {}
        left = rows_of[first : first + count, :]
        high = jnp.dot(left, g[:, 2 * W :], preferred_element_type=F32).astype(BF16)
        for e in (2, 3):
            out[first : first + count, e * W : (e + 1) * W] = high[:, (e - 2) * W : (e - 1) * W]
            got[NY - e] = send(slot(out, e, *rows), slot(into, NY - e, *rows), y_dev[e])
        low = jnp.dot(left, g[:, : 2 * W], preferred_element_type=F32)
        out[first : first + count, W : 2 * W] = low[:, W:].astype(BF16)
        got[3] = send(slot(out, 1, *rows), slot(into, 3, *rows), y_dev[1])
        return low[:, :W], got

    def u_sum(total, rows, into, got):
        first, count = rows
        for e in (1, 3, 2):
            got[e].wait_recv()
            total += into[first : first + count, e * W : (e + 1) * W].astype(F32)
        return total

    def v_product(left, rows, out, relay, into):
        first, count = rows[0], rows[1]
        def columns(begin, end):
            part = lax.dot_general(
                left, g[begin:end, :], (((1,), (1,)), ((), ())), preferred_element_type=F32
            )
            out[first : first + count, begin:end] = part.astype(BF16)
            return part

        columns(5 * W, NZ * W)
        got = {}
        half = count // 2
        for n, d, start in ((2, 2, first), (3, 6, first + half)):
            src = slot(out, PLACE[4], start, half)
            got[n] = send(src, relay.at[n, pl.ds(first, half), :], z_dev[d])
        for n, d, far in ((0, 1, 3), (1, 7, 5)):
            src = slot(out, PLACE[far], first, count)
            got[n] = send(src, relay.at[n, pl.ds(first, count), :], z_dev[d])
        part = columns(0, 5 * W)
        near = []
        for n, d in ((0, 1), (1, 7)):
            src = slot(out, PLACE[d], first, count)
            near.append(send(src, into.at[n, pl.ds(first, count), :], z_dev[d]))
        for n, d in ((0, 2), (1, 6)):
            kept[n, first : first + count] = part[:, PLACE[d] * W : (PLACE[d] + 1) * W]
        return part[:, :W], got, near

    def v_relay(stage, rows, relay, into, got, near):
        first, count = rows[0], rows[1]
        half = count // 2
        top, low = slice(first, first + half), slice(first + half, first + count)
        for n, d in ((0, 2), (1, 6)):
            got[n].wait_recv()
            got[n + 2].wait_recv()
            more = relay[n + 2, top, :].astype(F32)
            for part in (top, low):
                total = kept[n, part] + relay[n, part, :].astype(F32)
                if (part is top) == (n == 0):
                    total += more
                through[stage, n, part] = total.astype(BF16)
            src = through.at[stage, n, pl.ds(first, count), :]
            near.append(send(src, into.at[n + 2, pl.ds(first, count), :], z_dev[d]))

    def v_sum(total, rows, into, near):
        first, count = rows[0], rows[1]
        for n, copy in enumerate(near):
            copy.wait_recv()
            total += into[n, first : first + count, :].astype(F32)
        return total

    def of(rows):
        return slice(rows[0], rows[0] + rows[1])

    def mix(rows, first):
        return 3.4445 * x_ref[of(rows), :].astype(F32) - 4.775 * first

    def chunks(start, count, number):
        return [(start + n * (count // number), count // number) for n in range(number)]

    state = settled[0], mark[0], list(started)

    @pl.when(q == 0)
    def _():
        us = chunks(0, R, U_CHUNKS)
        u_in, ah_in = {}, {}
        for rows in us:
            acc[of(rows), :], u_in[rows] = u_product(xa, rows, su1, ru1)
        settle()
        for rows in us:
            first = u_sum(acc[of(rows), :], rows, ru1, u_in[rows])
            ah[of(rows), 0:W] = first.astype(BF16)
            ah_in[rows] = z_near(slot(ah, 0, *rows), ah, *rows)
            acc[of(rows), :] = mix(rows, first)
        settle()
        for rows in us:
            for d in (2, 6):
                ah_in[rows][d].wait_recv()
                z_far(ah, d, *rows, ah_in[rows])
        for rows in us:
            for d in (1, 7, 3, 5, (4, 2), (4, 6)):
                ah_in[rows][d].wait_recv()
            own_term, u_in[rows] = u_product(ah, rows, su2, ru2)
            acc[of(rows), :] += 2.0315 * own_term
        settle()
        for rows in us:
            second = u_sum(jnp.zeros((rows[1], W), F32), rows, ru2, u_in[rows])
            o_ref[of(rows), :] = (SCALE * (acc[of(rows), :] + 2.0315 * second)).astype(BF16)
        settle()
        settle()

    settled[0], mark[0] = state[:2]
    started[:] = state[2]

    @pl.when(q == 1)
    def _():
        vs = chunks(0, R, V_CHUNKS)
        v_in, av_in = {}, {}
        for rows in vs:
            acc[of(rows), :], *v_in[rows] = v_product(xb[of(rows), :], rows, ov1, rv1, fv1)
        settle()
        for rows in vs:
            v_relay(0, rows, rv1, fv1, *v_in[rows])
        for rows in vs:
            first = v_sum(acc[of(rows), :], rows, fv1, v_in[rows][1])
            av[of(rows), 0:W] = first.astype(BF16)
            av_in[rows] = [
                send(slot(av, 0, *rows), slot(av, NY - e, *rows), y_dev[e]) for e in (2, 1, 3)
            ]
            acc[of(rows), :] = mix(rows, first)
        settle()
        for rows in vs:
            for copy in av_in[rows]:
                copy.wait_recv()
            own_term, *v_in[rows] = v_product(av[of(rows), :], rows, ov2, rv2, fv2)
            acc[of(rows), :] += 2.0315 * own_term
        settle()
        for rows in vs:
            v_relay(1, rows, rv2, fv2, *v_in[rows])
        for rows in vs:
            second = v_sum(jnp.zeros((rows[1], W), F32), rows, fv2, v_in[rows][1])
            o_ref[of(rows), :] = (SCALE * (acc[of(rows), :] + 2.0315 * second)).astype(BF16)
        settle()
        settle()


COPIES = 192


def body(iterate):
    return pl.pallas_call(
        kernel,
        out_shape=jax.ShapeDtypeStruct((R, W), BF16),
        in_specs=[pl.BlockSpec(memory_space=pl.ANY)],
        out_specs=pl.BlockSpec(memory_space=pltpu.VMEM),
        scratch_shapes=[
            pltpu.VMEM((R, W), BF16),
            pltpu.VMEM((R, NZ * W), BF16),
            pltpu.VMEM((R, NY * W), BF16),
            pltpu.VMEM((R, NZ * W), BF16),
            pltpu.VMEM((R, NY * W), BF16),
            pltpu.VMEM((NZ * W, 2 * W), BF16),
            pltpu.VMEM((7, NZ * W // 8, 2 * W), BF16),
            pltpu.VMEM((NZ * W, NY * W), BF16),
            pltpu.VMEM((R, NY * W), BF16),
            pltpu.VMEM((R, NY * W), BF16),
            pltpu.VMEM((R, NY * W), BF16),
            pltpu.VMEM((R, NY * W), BF16),
            pltpu.VMEM((R, NZ * W), BF16),
            pltpu.VMEM((4, R, W), BF16),
            pltpu.VMEM((4, R, W), BF16),
            pltpu.VMEM((R, NZ * W), BF16),
            pltpu.VMEM((4, R, W), BF16),
            pltpu.VMEM((4, R, W), BF16),
            pltpu.VMEM((R, NZ * W), BF16),
            pltpu.VMEM((R, NY * W), BF16),
            pltpu.VMEM((2, R, W), F32),
            pltpu.VMEM((2, 2, R, W), BF16),
            pltpu.VMEM((R, W), F32),
            pltpu.SemaphoreType.DMA,
            pltpu.SemaphoreType.DMA((COPIES,)),
            pltpu.SemaphoreType.DMA((COPIES,)),
        ],
        compiler_params=pltpu.CompilerParams(
            collective_id=0, has_side_effects=True, vmem_limit_bytes=32 << 20
        ),
        name="newton_schulz",
    )(iterate)


def solution(mesh):
    placed = (P("row", "col"),)
    return jax.shard_map(
        body, mesh=mesh, in_specs=placed, out_specs=P("row", "col"), check_vma=False
    )
```
